32 devices in a mesh: samp: 4 (over z), feat: 8 (over y, x, core).
Axes of the slice: x: 2, y: 2, z: 4, core: 2. Of those that a mesh axis runs over, the one named last changes fastest.
Arguments:
- design: bfloat16 [6144, 8192], P('samp', 'feat'), may hold values from -6 to 6
- labels: int32 [6144], P('samp'), may hold values 0 or 1
- coef_all: float32 [1048576], replicated, may hold values from -0.13 to 0.13
- active: int32 [8192], P('feat'), may hold values from 0 to 1048575, as said below
- penalty: float32 [8192], P('feat'), may hold values from 4 to 40
Outputs:
- gram: float32 [8192, 8192], P('samp', 'feat')
- gradient: float32 [8192], P('feat')
The draws below stay inside these ranges and needn't reach their ends.
Inputs may be any that keep to these rules, and one draw needn't show every extreme that they name: `active`: the indices are distinct.
All inputs are finite; a program needn't handle non-finite values. No bound on the sum of `labels` on one device may be relied on, other than what follows from the above.
Results may differ from the reference program's by a relative error of at most 0.003.
Values may be sent and summed in bfloat16 or wider, within the bound.
A program may use at most 128 MiB of HBM per device.

```python
import math
import jax
import jax.numpy as jnp
from jax import lax

A = 8192
POOL = 1048576
N = 6144


def draw_active(key, part):
    return jax.random.permutation(key, POOL)[:A].astype(jnp.int32)


def with_ends(array, stream_key, smallest, high):
    place = [jax.random.randint(jax.random.fold_in(stream_key, axis), (), 0, length) for axis, length in enumerate(array.shape)]
    widest = array.shape.index(max(array.shape))
    beside = place[:widest] + [(place[widest] + 1) % array.shape[widest]] + place[widest + 1:]
    return array.at[tuple(place)].set(smallest).at[tuple(beside)].set(high)


def block_levels(key, extent, split, least, top_value):
    def one(axis_at, blocks):
        heights = jax.random.uniform(jax.random.fold_in(jax.random.fold_in(key, 6), axis_at), (blocks,), jnp.float32, least / len(split), top_value / len(split))
        return jnp.repeat(jnp.exp(heights), extent[axis_at] // blocks).reshape((-1,) + (1,) * (len(extent) - axis_at - 1))

    loudness = one(*split[0])
    for cut in split[1:]:
        loudness = loudness * one(*cut)
    return loudness


def normal_values(own_key, dims, spread, reach, shards=(), kind=jnp.bfloat16):
    entries = jax.random.normal(own_key, dims, jnp.float32) * spread
    if len(shards) > 0:
        entries = block_levels(own_key, dims, shards, -0.22, 0.18) * entries
    return jnp.clip(entries, min=-reach, max=reach).astype(kind)


def setup_inputs(seed: int = 0) -> dict:
    splits = jax.random.split(jax.random.key(seed), 6)
    design = normal_values(splits[0], (N, A), 1.0, 6.0, ((0, 4), (1, 8)))
    labels = with_ends((jax.random.randint(splits[1], (N,), 0, 2) < 1).astype(jnp.int32), jax.random.fold_in(splits[1], 1), 0, 1)
    coef_all = normal_values(splits[2], (POOL,), 0.022, 0.13, (), jnp.float32)
    active = draw_active(jax.random.fold_in(splits[5], 71), 0)
    penalty = jnp.clip(jnp.exp(math.log(40.0) - 2.3025851 * jax.random.uniform(splits[4], (A,), jnp.float32) ** block_levels(splits[4], (A,), ((0, 8),), -0.2, 0.2)), 4.0, 40.0)
    return dict(design=design, labels=labels, coef_all=coef_all, active=active, penalty=penalty)


def reference(design, labels, coef_all, active, penalty):
    beta = coef_all[active]
    beta_b = beta.astype(jnp.bfloat16)
    margin = jnp.dot(design, beta_b, preferred_element_type=jnp.float32)
    prob = 1.0 / (1.0 + jnp.exp(-margin))
    weight = prob * (1.0 - prob)
    resid = prob - labels.astype(jnp.float32)
    weighted = (design.astype(jnp.float32) * weight[:, None]).astype(jnp.bfloat16)
    resid_b = resid.astype(jnp.bfloat16)
    scale = 1.0 / jnp.sqrt(jnp.float32(N))
    gram = lax.dot_general(design.astype(jnp.float32), weighted.astype(jnp.float32), (((0,), (0,)), ((), ())), preferred_element_type=jnp.float32) * scale
    grad_data = jnp.dot(resid_b, design, preferred_element_type=jnp.float32) * scale
    gradient = grad_data + penalty * beta
    return (gram, gradient)
```

```python
import jax
import jax.numpy as jnp
from jax import lax
from jax.sharding import PartitionSpec as P


def per_device(design, labels, coef_all, active, penalty):
    rows = design.shape[0]
    total_rows = rows * lax.axis_size("samp")
    scale = 1.0 / jnp.sqrt(jnp.float32(total_rows))
    beta = coef_all[active]
    partial_margin = jnp.dot(design, beta.astype(jnp.bfloat16), preferred_element_type=jnp.float32)
    margin = lax.psum(partial_margin, "feat")
    prob = 1.0 / (1.0 + jnp.exp(-margin))
    weight = prob * (1.0 - prob)
    resid = prob - labels.astype(jnp.float32)
    weighted = (design.astype(jnp.float32) * weight[:, None]).astype(jnp.bfloat16)
    resid_b = resid.astype(jnp.bfloat16)
    grad_part = jnp.dot(resid_b, design, preferred_element_type=jnp.float32)
    gradient = lax.psum(grad_part, "samp") * scale + penalty * beta
    terms = lax.dot_general(
        lax.all_gather(design, "feat", axis=1, tiled=True),
        weighted,
        (((0,), (0,)), ((), ())),
        preferred_element_type=jnp.float32,
    )
    gram = lax.psum_scatter(terms.astype(jnp.bfloat16), "samp", scatter_dimension=0, tiled=True).astype(jnp.float32) * scale
    return (gram, gradient)


def solution(mesh):
    in_specs = (P("samp", "feat"), P("samp"), P(), P("feat"), P("feat"))
    out_specs = (P("samp", "feat"), P("feat"))
    return jax.shard_map(
        per_device, mesh=mesh, in_specs=in_specs, out_specs=out_specs, check_vma=False
    )
```

```python
import functools

import jax
import jax.numpy as jnp
from jax import lax
from jax.experimental import pallas as pl
from jax.experimental.pallas import tpu as pltpu
from jax.sharding import PartitionSpec as P

MESH = pl.DeviceIdType.MESH


def kernel(nz, nc, nch, x_ref, w_ref, r_ref, acc_ref, grad_ref, col, row, wt,
           own_sem, z_send, z_recv, ring_send, ring_recv, sib_send, sib_recv, loc_sem):
    s = lax.axis_index("samp")
    f = lax.axis_index("feat")
    c, k = f // 2, f % 2

    def flip(p):
        return jnp.where(p < nc // 2, p, 3 * nc // 2 - 1 - p)

    pos = flip(c)
    d = lax.rem(pos - flip(s) + nc, nc)
    nxt = (s, 2 * flip(lax.rem(pos + 1, nc)) + k)
    prv = (s, 2 * flip(lax.rem(pos + nc - 1, nc)) + k)
    sib = (s, 2 * c + 1 - k)
    width = wt.shape[1]
    tile = min(256, width)

    own = pltpu.make_async_copy(x_ref, col.at[s], own_sem)
    own.start()
    acc_ref[...] = jnp.zeros_like(acc_ref)
    grad_ref[...] = jnp.zeros_like(grad_ref)

    barrier = pltpu.get_barrier_semaphore()
    for dev in (nxt, prv, sib):
        pl.semaphore_signal(barrier, inc=1, device_id=dev, device_id_type=MESH)

    @pl.when(s > 0)
    def _():
        pl.semaphore_signal(barrier, inc=1, device_id=(s - 1, f), device_id_type=MESH)

    @pl.when(s < nz - 1)
    def _():
        pl.semaphore_signal(barrier, inc=1, device_id=(s + 1, f), device_id_type=MESH)

    pl.semaphore_wait(barrier, 3 + (s > 0).astype(jnp.int32) + (s < nz - 1).astype(jnp.int32))
    own.wait()

    def z_copy(o, i, way):
        return pltpu.make_async_remote_copy(
            col.at[o, i], col.at[o, i], z_send.at[o, i, way], z_recv.at[o, i],
            device_id=(s + 1 - 2 * way, f), device_id_type=MESH)

    def ring_copy(src, o, i, dev):
        return pltpu.make_async_remote_copy(
            src.at[o, i], row.at[k, o, i], ring_send.at[o, i], ring_recv.at[o, i],
            device_id=dev, device_id_type=MESH)

    def sib_copy(src, o, i):
        return pltpu.make_async_remote_copy(
            src.at[o, i], row.at[k, o, i], sib_send.at[o, i], sib_recv.at[o, i],
            device_id=sib, device_id_type=MESH)

    def sib_wait(o, i):
        pltpu.make_async_remote_copy(
            row.at[1 - k, o, i], row.at[1 - k, o, i], sib_send.at[o, i], sib_recv.at[o, i],
            device_id=sib, device_id_type=MESH).wait_recv()

    def loc_copy(o, i):
        return pltpu.make_async_copy(col.at[o, i], row.at[k, o, i], loc_sem.at[o, i])

    def send_own(i):
        @pl.when(s < nz - 1)
        def _():
            z_copy(s, i, 0).start()

        @pl.when(s > 0)
        def _():
            z_copy(s, i, 1).start()

    def is_cw(o, i):
        return lax.rem(i + (o > s).astype(jnp.int32), 2) == 0

    def spread(o, i):
        @pl.when(d == 0)
        def _():
            cw = is_cw(o, i)

            @pl.when(cw)
            def _():
                ring_copy(col, o, i, nxt).start()

            @pl.when(jnp.logical_not(cw))
            def _():
                ring_copy(col, o, i, prv).start()

            sib_copy(col, o, i).start()
            loc_copy(o, i).start()

    def passing(o, i, cw):
        @pl.when(is_cw(o, i) == cw)
        def _():
            mine = row.at[k]
            ring_copy(mine, o, i, nxt).wait_recv()
            if cw:
                @pl.when(d < nc - 1)
                def _():
                    ring_copy(mine, o, i, nxt).start()
            else:
                @pl.when(d > 1)
                def _():
                    ring_copy(mine, o, i, prv).start()
            sib_copy(mine, o, i).start()

    def compute(o, i):
        sib_wait(o, i)

        @pl.when(d == 0)
        def _():
            loc_copy(o, i).wait()

        block = col[o, i]
        wt[...] = (block.astype(jnp.float32) * w_ref[o, i]).astype(jnp.bfloat16)
        grad_ref[...] += jnp.dot(r_ref[o, i], block, preferred_element_type=jnp.float32)
        for kk in range(2):
            @pl.loop(0, width // tile)
            def _(m):
                at = pl.multiple_of(m * tile, tile)
                lhs = row[kk, o, i, :, pl.ds(at, tile)]
                acc_ref[pl.ds(kk * width + at, tile), :] += lax.dot_general(
                    lhs, wt[...], (((0,), (0,)), ((), ())), preferred_element_type=jnp.float32)

    steps = (nz - 1) * nch

    def events(e, fn):
        @pl.when(jnp.logical_and(e >= 0, e < steps))
        def _():
            j = e // nch + 1
            i = e % nch

            @pl.when(j == 1)
            def _():
                fn(s, i)

            @pl.when(s - j >= 0)
            def _():
                fn(s - j, i)

            @pl.when(s + j < nz)
            def _():
                fn(s + j, i)

    def arrive(o, i):
        @pl.when(o != s)
        def _():
            z_copy(o, i, 0).wait_recv()

            @pl.when(jnp.logical_and(o < s, s < nz - 1))
            def _():
                z_copy(o, i, 0).start()

            @pl.when(jnp.logical_and(o > s, s > 0))
            def _():
                z_copy(o, i, 1).start()
        spread(o, i)

    send_own(0)

    @pl.loop(0, steps + nc)
    def _(t):
        @pl.when(t + 1 < nch)
        def _():
            send_own(t + 1)
        events(t, arrive)

        @pl.when(d > 0)
        def _():
            events(t - d, lambda o, i: passing(o, i, True))
            events(t - (nc - d), lambda o, i: passing(o, i, False))
        events(t - nc, compute)

    @pl.loop(0, nz * nch)
    def _(q):
        o = q // nch
        i = q % nch

        @pl.when(jnp.logical_and(o <= s, s < nz - 1))
        def _():
            z_copy(o, i, 0).wait_send()

        @pl.when(jnp.logical_and(o >= s, s > 0))
        def _():
            z_copy(o, i, 1).wait_send()

        sib_copy(row.at[k], o, i).wait_send()
        cw = is_cw(o, i)

        @pl.when(jnp.logical_or(jnp.logical_and(cw, d < nc - 1),
                                jnp.logical_and(jnp.logical_not(cw), d != 1)))
        def _():
            ring_copy(row.at[k], o, i, nxt).wait_send()


def per_device(nz, nf, design, labels, coef_all, active, penalty):
    rows, width = design.shape
    nc = nf // 2
    nch = 6
    ch = rows // nch
    scale = 1.0 / jnp.sqrt(jnp.float32(rows * nz))
    beta = coef_all[active]
    partial_margin = jnp.dot(design, beta.astype(jnp.bfloat16), preferred_element_type=jnp.float32)
    margin = lax.psum(partial_margin, "feat")
    prob = 1.0 / (1.0 + jnp.exp(-margin))
    weight = prob * (1.0 - prob)
    resid = prob - labels.astype(jnp.float32)
    both = lax.all_gather(jnp.stack([weight, resid]), "samp", axis=0)
    w4 = both[:, 0].reshape(nz, nch, ch, 1)
    r4 = jnp.broadcast_to(both[:, 1].astype(jnp.bfloat16).reshape(nz, nch, 1, ch), (nz, nch, 16, ch))
    vmem = pl.BlockSpec(memory_space=pltpu.VMEM)
    dma = pltpu.SemaphoreType.DMA
    terms, grad = pl.pallas_call(
        functools.partial(kernel, nz, nc, nch),
        out_shape=(jax.ShapeDtypeStruct((2 * width, width), jnp.float32),
                   jax.ShapeDtypeStruct((16, width), jnp.float32)),
        in_specs=[pl.BlockSpec(memory_space=pl.ANY), vmem, vmem],
        out_specs=(vmem, vmem),
        scratch_shapes=[
            pltpu.VMEM((nz, nch, ch, width), jnp.bfloat16),
            pltpu.VMEM((2, nz, nch, ch, width), jnp.bfloat16),
            pltpu.VMEM((ch, width), jnp.bfloat16),
            dma,
            dma((nz, nch, 2)),
            dma((nz, nch)),
            dma((nz, nch)),
            dma((nz, nch)),
            dma((nz, nch)),
            dma((nz, nch)),
            dma((nz, nch)),
        ],
        compiler_params=pltpu.CompilerParams(
            collective_id=0, has_side_effects=True, vmem_limit_bytes=60 * 1024 * 1024),
        cost_estimate=pl.CostEstimate(
            flops=4 * nz * rows * width * width, bytes_accessed=2 * rows * width + 8 * width * width,
            transcendentals=0),
    )(design.reshape(nch, ch, width), w4, r4)
    return terms * scale, grad[0] * scale + penalty * beta


def solution(mesh):
    in_specs = (P("samp", "feat"), P("samp"), P(), P("feat"), P("feat"))
    out_specs = (P("samp", "feat"), P("feat"))
    return jax.shard_map(
        functools.partial(per_device, mesh.shape["samp"], mesh.shape["feat"]),
        mesh=mesh, in_specs=in_specs, out_specs=out_specs, check_vma=False
    )
```

```python
import functools

import jax
import jax.numpy as jnp
from jax import lax
from jax.experimental import pallas as pl
from jax.experimental.pallas import tpu as pltpu
from jax.sharding import PartitionSpec as P

MESH = pl.DeviceIdType.MESH


def kernel(nz, nc, nch, x_ref, w_ref, r_ref, acc_ref, grad_ref, col, row, wt,
           own_sem, z_send, z_recv, ring_send, ring_recv, sib_send, sib_recv, loc_sem):
    s = lax.axis_index("samp")
    f = lax.axis_index("feat")
    c, k = f // 2, f % 2

    def flip(p):
        return jnp.where(p < nc // 2, p, 3 * nc // 2 - 1 - p)

    pos = flip(c)
    d = lax.rem(pos - flip(s) + nc, nc)
    nxt = (s, 2 * flip(lax.rem(pos + 1, nc)) + k)
    prv = (s, 2 * flip(lax.rem(pos + nc - 1, nc)) + k)
    sib = (s, 2 * c + 1 - k)
    width = wt.shape[1]
    tile = min(256, width)

    own = pltpu.make_async_copy(x_ref, col.at[s], own_sem)
    own.start()
    acc_ref[...] = jnp.zeros_like(acc_ref)
    grad_ref[...] = jnp.zeros_like(grad_ref)

    barrier = pltpu.get_barrier_semaphore()
    for dev in (nxt, prv, sib):
        pl.semaphore_signal(barrier, inc=1, device_id=dev, device_id_type=MESH)

    @pl.when(s > 0)
    def _():
        pl.semaphore_signal(barrier, inc=1, device_id=(s - 1, f), device_id_type=MESH)

    @pl.when(s < nz - 1)
    def _():
        pl.semaphore_signal(barrier, inc=1, device_id=(s + 1, f), device_id_type=MESH)

    pl.semaphore_wait(barrier, 3 + (s > 0).astype(jnp.int32) + (s < nz - 1).astype(jnp.int32))
    own.wait()

    def z_copy(o, i, way):
        return pltpu.make_async_remote_copy(
            col.at[o, i], col.at[o, i], z_send.at[o, i, way], z_recv.at[o, i],
            device_id=(s + 1 - 2 * way, f), device_id_type=MESH)

    def ring_copy(src, o, i, dev):
        return pltpu.make_async_remote_copy(
            src.at[o, i], row.at[k, o, i], ring_send.at[o, i], ring_recv.at[o, i],
            device_id=dev, device_id_type=MESH)

    def sib_copy(src, o, i):
        return pltpu.make_async_remote_copy(
            src.at[o, i], row.at[k, o, i], sib_send.at[o, i], sib_recv.at[o, i],
            device_id=sib, device_id_type=MESH)

    def sib_wait(o, i):
        pltpu.make_async_remote_copy(
            row.at[1 - k, o, i], row.at[1 - k, o, i], sib_send.at[o, i], sib_recv.at[o, i],
            device_id=sib, device_id_type=MESH).wait_recv()

    def loc_copy(o, i):
        return pltpu.make_async_copy(col.at[o, i], row.at[k, o, i], loc_sem.at[o, i])

    def send_own(i):
        @pl.when(s < nz - 1)
        def _():
            z_copy(s, i, 0).start()

        @pl.when(s > 0)
        def _():
            z_copy(s, i, 1).start()

    def is_cw(o, i):
        return lax.rem(i + (o > s).astype(jnp.int32), 2) == 0

    def spread(o, i):
        @pl.when(d == 0)
        def _():
            cw = is_cw(o, i)

            @pl.when(cw)
            def _():
                ring_copy(col, o, i, nxt).start()

            @pl.when(jnp.logical_not(cw))
            def _():
                ring_copy(col, o, i, prv).start()

            sib_copy(col, o, i).start()
            loc_copy(o, i).start()

    def passing(o, i, cw):
        @pl.when(is_cw(o, i) == cw)
        def _():
            mine = row.at[k]
            ring_copy(mine, o, i, nxt).wait_recv()
            if cw:
                @pl.when(d < nc - 1)
                def _():
                    ring_copy(mine, o, i, nxt).start()
            else:
                @pl.when(d > 1)
                def _():
                    ring_copy(mine, o, i, prv).start()
            sib_copy(mine, o, i).start()

    def compute(o, i):
        sib_wait(o, i)

        @pl.when(d == 0)
        def _():
            loc_copy(o, i).wait()

        block = col[o, i]
        wt[...] = (block.astype(jnp.float32) * w_ref[o, i]).astype(jnp.bfloat16)
        grad_ref[...] += jnp.dot(r_ref[o, i], block, preferred_element_type=jnp.float32)
        for kk in range(2):
            @pl.loop(0, width // tile)
            def _(m):
                at = pl.multiple_of(m * tile, tile)
                lhs = row[kk, o, i, :, pl.ds(at, tile)]
                acc_ref[pl.ds(kk * width + at, tile), :] += lax.dot_general(
                    lhs, wt[...], (((0,), (0,)), ((), ())), preferred_element_type=jnp.float32)

    steps = (nz - 1) * nch

    def events(e, fn):
        @pl.when(jnp.logical_and(e >= 0, e < steps))
        def _():
            j = e // nch + 1
            i = e % nch

            @pl.when(j == 1)
            def _():
                fn(s, i)

            @pl.when(s - j >= 0)
            def _():
                fn(s - j, i)

            @pl.when(s + j < nz)
            def _():
                fn(s + j, i)

    def arrive(o, i):
        @pl.when(o != s)
        def _():
            z_copy(o, i, 0).wait_recv()

            @pl.when(jnp.logical_and(o < s, s < nz - 1))
            def _():
                z_copy(o, i, 0).start()

            @pl.when(jnp.logical_and(o > s, s > 0))
            def _():
                z_copy(o, i, 1).start()
        spread(o, i)

    send_own(0)

    @pl.loop(0, steps + nc)
    def _(t):
        @pl.when(t + 1 < nch)
        def _():
            send_own(t + 1)
        events(t, arrive)

        @pl.when(d > 0)
        def _():
            events(t - d, lambda o, i: passing(o, i, True))
            events(t - (nc - d), lambda o, i: passing(o, i, False))
        events(t - nc, compute)

    @pl.loop(0, nz * nch)
    def _(q):
        o = q // nch
        i = q % nch

        @pl.when(jnp.logical_and(o <= s, s < nz - 1))
        def _():
            z_copy(o, i, 0).wait_send()

        @pl.when(jnp.logical_and(o >= s, s > 0))
        def _():
            z_copy(o, i, 1).wait_send()

        sib_copy(row.at[k], o, i).wait_send()
        cw = is_cw(o, i)

        @pl.when(jnp.logical_or(jnp.logical_and(cw, d < nc - 1),
                                jnp.logical_and(jnp.logical_not(cw), d != 1)))
        def _():
            ring_copy(row.at[k], o, i, nxt).wait_send()


def per_device(nz, nf, design, labels, coef_all, active, penalty):
    rows, width = design.shape
    nc = nf // 2
    nch = 12
    ch = rows // nch
    scale = 1.0 / jnp.sqrt(jnp.float32(rows * nz))
    beta = coef_all[active]
    partial_margin = jnp.dot(design, beta.astype(jnp.bfloat16), preferred_element_type=jnp.float32)
    margin = lax.psum(partial_margin, "feat")
    prob = 1.0 / (1.0 + jnp.exp(-margin))
    weight = prob * (1.0 - prob)
    resid = prob - labels.astype(jnp.float32)
    both = lax.all_gather(jnp.stack([weight, resid]), "samp", axis=0)
    w4 = both[:, 0].reshape(nz, nch, ch, 1)
    r4 = jnp.broadcast_to(both[:, 1].astype(jnp.bfloat16).reshape(nz, nch, 1, ch), (nz, nch, 16, ch))
    vmem = pl.BlockSpec(memory_space=pltpu.VMEM)
    dma = pltpu.SemaphoreType.DMA
    terms, grad = pl.pallas_call(
        functools.partial(kernel, nz, nc, nch),
        out_shape=(jax.ShapeDtypeStruct((2 * width, width), jnp.float32),
                   jax.ShapeDtypeStruct((16, width), jnp.float32)),
        in_specs=[pl.BlockSpec(memory_space=pl.ANY), vmem, vmem],
        out_specs=(vmem, vmem),
        scratch_shapes=[
            pltpu.VMEM((nz, nch, ch, width), jnp.bfloat16),
            pltpu.VMEM((2, nz, nch, ch, width), jnp.bfloat16),
            pltpu.VMEM((ch, width), jnp.bfloat16),
            dma,
            dma((nz, nch, 2)),
            dma((nz, nch)),
            dma((nz, nch)),
            dma((nz, nch)),
            dma((nz, nch)),
            dma((nz, nch)),
            dma((nz, nch)),
        ],
        compiler_params=pltpu.CompilerParams(
            collective_id=0, has_side_effects=True, vmem_limit_bytes=60 * 1024 * 1024),
        cost_estimate=pl.CostEstimate(
            flops=4 * nz * rows * width * width, bytes_accessed=2 * rows * width + 8 * width * width,
            transcendentals=0),
    )(design.reshape(nch, ch, width), w4, r4)
    return terms * scale, grad[0] * scale + penalty * beta


def solution(mesh):
    in_specs = (P("samp", "feat"), P("samp"), P(), P("feat"), P("feat"))
    out_specs = (P("samp", "feat"), P("feat"))
    return jax.shard_map(
        functools.partial(per_device, mesh.shape["samp"], mesh.shape["feat"]),
        mesh=mesh, in_specs=in_specs, out_specs=out_specs, check_vma=False
    )
```

```python
import functools

import jax
import jax.numpy as jnp
from jax import lax
from jax.experimental import pallas as pl
from jax.experimental.pallas import tpu as pltpu
from jax.sharding import PartitionSpec as P

MESH = pl.DeviceIdType.MESH


def kernel(nz, nc, nch, x_ref, w_ref, r_ref, acc_ref, grad_ref, col, row, wt,
           own_sem, z_send, z_recv, ring_send, ring_recv, sib_send, sib_recv, loc_sem):
    s = lax.axis_index("samp")
    f = lax.axis_index("feat")
    c, k = f // 2, f % 2

    def flip(p):
        return jnp.where(p < nc // 2, p, 3 * nc // 2 - 1 - p)

    pos = flip(c)
    d = lax.rem(pos - flip(s) + nc, nc)
    nxt = (s, 2 * flip(lax.rem(pos + 1, nc)) + k)
    prv = (s, 2 * flip(lax.rem(pos + nc - 1, nc)) + k)
    sib = (s, 2 * c + 1 - k)
    depth, width = wt.shape
    tile = min(256, width)

    own = pltpu.make_async_copy(x_ref, col.at[s], own_sem)
    own.start()
    acc_ref[...] = jnp.zeros_like(acc_ref)
    grad_ref[...] = jnp.zeros_like(grad_ref)

    barrier = pltpu.get_barrier_semaphore()
    for dev in (nxt, prv, sib):
        pl.semaphore_signal(barrier, inc=1, device_id=dev, device_id_type=MESH)

    @pl.when(s > 0)
    def _():
        pl.semaphore_signal(barrier, inc=1, device_id=(s - 1, f), device_id_type=MESH)

    @pl.when(s < nz - 1)
    def _():
        pl.semaphore_signal(barrier, inc=1, device_id=(s + 1, f), device_id_type=MESH)

    pl.semaphore_wait(barrier, 3 + (s > 0).astype(jnp.int32) + (s < nz - 1).astype(jnp.int32))
    own.wait()

    def z_copy(o, i, way):
        return pltpu.make_async_remote_copy(
            col.at[o, i], col.at[o, i], z_send.at[o, i, way], z_recv.at[o, i],
            device_id=(s + 1 - 2 * way, f), device_id_type=MESH)

    def ring_copy(src, o, i, dev):
        return pltpu.make_async_remote_copy(
            src.at[o, i], row.at[k, o, i], ring_send.at[o, i], ring_recv.at[o, i],
            device_id=dev, device_id_type=MESH)

    def sib_copy(src, o, i):
        return pltpu.make_async_remote_copy(
            src.at[o, i], row.at[k, o, i], sib_send.at[o, i], sib_recv.at[o, i],
            device_id=sib, device_id_type=MESH)

    def sib_wait(o, i):
        pltpu.make_async_remote_copy(
            row.at[1 - k, o, i], row.at[1 - k, o, i], sib_send.at[o, i], sib_recv.at[o, i],
            device_id=sib, device_id_type=MESH).wait_recv()

    def loc_copy(o, i):
        return pltpu.make_async_copy(col.at[o, i], row.at[k, o, i], loc_sem.at[o, i])

    def send_own(i):
        @pl.when(s < nz - 1)
        def _():
            z_copy(s, i, 0).start()

        @pl.when(s > 0)
        def _():
            z_copy(s, i, 1).start()

    def is_cw(o, i):
        return lax.rem(i + (o > s).astype(jnp.int32), 2) == 0

    def spread(o, i):
        @pl.when(d == 0)
        def _():
            cw = is_cw(o, i)

            @pl.when(cw)
            def _():
                ring_copy(col, o, i, nxt).start()

            @pl.when(jnp.logical_not(cw))
            def _():
                ring_copy(col, o, i, prv).start()

            sib_copy(col, o, i).start()
            loc_copy(o, i).start()

    def passing(o, i, cw):
        @pl.when(is_cw(o, i) == cw)
        def _():
            mine = row.at[k]
            ring_copy(mine, o, i, nxt).wait_recv()
            if cw:
                @pl.when(d < nc - 1)
                def _():
                    ring_copy(mine, o, i, nxt).start()
            else:
                @pl.when(d > 1)
                def _():
                    ring_copy(mine, o, i, prv).start()
            sib_copy(mine, o, i).start()

    def compute(o, i):
        sib_wait(o, i)

        @pl.when(d == 0)
        def _():
            loc_copy(o, i).wait()

        @pl.when(i % 2 == 1)
        def _():
            pair = pl.ds(i - 1, 2)
            block = col[o, pair].reshape(depth, width)
            wt[...] = (block.astype(jnp.float32) * w_ref[o, i // 2]).astype(jnp.bfloat16)
            grad_ref[...] += jnp.dot(r_ref[o, i // 2], block, preferred_element_type=jnp.float32)
            for kk in range(2):
                @pl.loop(0, width // tile)
                def _(m):
                    at = pl.multiple_of(m * tile, tile)
                    lhs = row[kk, o, pair, :, pl.ds(at, tile)].reshape(depth, tile)
                    acc_ref[pl.ds(kk * width + at, tile), :] += lax.dot_general(
                        lhs, wt[...], (((0,), (0,)), ((), ())), preferred_element_type=jnp.float32)

    steps = (nz - 1) * nch

    def events(e, fn):
        @pl.when(jnp.logical_and(e >= 0, e < steps))
        def _():
            j = e // nch + 1
            i = e % nch

            @pl.when(j == 1)
            def _():
                fn(s, i)

            @pl.when(s - j >= 0)
            def _():
                fn(s - j, i)

            @pl.when(s + j < nz)
            def _():
                fn(s + j, i)

    def arrive(o, i):
        @pl.when(o != s)
        def _():
            z_copy(o, i, 0).wait_recv()

            @pl.when(jnp.logical_and(o < s, s < nz - 1))
            def _():
                z_copy(o, i, 0).start()

            @pl.when(jnp.logical_and(o > s, s > 0))
            def _():
                z_copy(o, i, 1).start()
        spread(o, i)

    send_own(0)
    send_own(1)

    @pl.loop(0, steps + nc)
    def _(t):
        @pl.when(t + 2 < nch)
        def _():
            send_own(t + 2)
        events(t, arrive)

        @pl.when(d > 0)
        def _():
            events(t - d, lambda o, i: passing(o, i, True))
            events(t - (nc - d), lambda o, i: passing(o, i, False))
        events(t - nc, compute)

    @pl.loop(0, nz * nch)
    def _(q):
        o = q // nch
        i = q % nch

        @pl.when(jnp.logical_and(o <= s, s < nz - 1))
        def _():
            z_copy(o, i, 0).wait_send()

        @pl.when(jnp.logical_and(o >= s, s > 0))
        def _():
            z_copy(o, i, 1).wait_send()

        sib_copy(row.at[k], o, i).wait_send()
        cw = is_cw(o, i)

        @pl.when(jnp.logical_or(jnp.logical_and(cw, d < nc - 1),
                                jnp.logical_and(jnp.logical_not(cw), d != 1)))
        def _():
            ring_copy(row.at[k], o, i, nxt).wait_send()


def per_device(nz, nf, design, labels, coef_all, active, penalty):
    rows, width = design.shape
    nc = nf // 2
    nch = 12
    ch = rows // nch
    scale = 1.0 / jnp.sqrt(jnp.float32(rows * nz))
    beta = coef_all[active]
    partial_margin = jnp.dot(design, beta.astype(jnp.bfloat16), preferred_element_type=jnp.float32)
    margin = lax.psum(partial_margin, "feat")
    prob = 1.0 / (1.0 + jnp.exp(-margin))
    weight = prob * (1.0 - prob)
    resid = prob - labels.astype(jnp.float32)
    both = lax.all_gather(jnp.stack([weight, resid]), "samp", axis=0)
    w4 = both[:, 0].reshape(nz, nch // 2, 2 * ch, 1)
    r4 = jnp.broadcast_to(both[:, 1].astype(jnp.bfloat16).reshape(nz, nch // 2, 1, 2 * ch), (nz, nch // 2, 16, 2 * ch))
    vmem = pl.BlockSpec(memory_space=pltpu.VMEM)
    dma = pltpu.SemaphoreType.DMA
    terms, grad = pl.pallas_call(
        functools.partial(kernel, nz, nc, nch),
        out_shape=(jax.ShapeDtypeStruct((2 * width, width), jnp.float32),
                   jax.ShapeDtypeStruct((16, width), jnp.float32)),
        in_specs=[pl.BlockSpec(memory_space=pl.ANY), vmem, vmem],
        out_specs=(vmem, vmem),
        scratch_shapes=[
            pltpu.VMEM((nz, nch, ch, width), jnp.bfloat16),
            pltpu.VMEM((2, nz, nch, ch, width), jnp.bfloat16),
            pltpu.VMEM((2 * ch, width), jnp.bfloat16),
            dma,
            dma((nz, nch, 2)),
            dma((nz, nch)),
            dma((nz, nch)),
            dma((nz, nch)),
            dma((nz, nch)),
            dma((nz, nch)),
            dma((nz, nch)),
        ],
        compiler_params=pltpu.CompilerParams(
            collective_id=0, has_side_effects=True, vmem_limit_bytes=60 * 1024 * 1024),
        cost_estimate=pl.CostEstimate(
            flops=4 * nz * rows * width * width, bytes_accessed=2 * rows * width + 8 * width * width,
            transcendentals=0),
    )(design.reshape(nch, ch, width), w4, r4)
    return terms * scale, grad[0] * scale + penalty * beta


def solution(mesh):
    in_specs = (P("samp", "feat"), P("samp"), P(), P("feat"), P("feat"))
    out_specs = (P("samp", "feat"), P("feat"))
    return jax.shard_map(
        functools.partial(per_device, mesh.shape["samp"], mesh.shape["feat"]),
        mesh=mesh, in_specs=in_specs, out_specs=out_specs, check_vma=False
    )
```

```python
import functools

import jax
import jax.numpy as jnp
from jax import lax
from jax.experimental import pallas as pl
from jax.experimental.pallas import tpu as pltpu
from jax.sharding import PartitionSpec as P

MESH = pl.DeviceIdType.MESH


def kernel(nz, nc, nch, x_ref, w_ref, r_ref, acc_ref, grad_ref, col, row, wt,
           own_sem, z_send, z_recv, ring_send, ring_recv, sib_send, sib_recv, loc_sem):
    s = lax.axis_index("samp")
    f = lax.axis_index("feat")
    c, k = f // 2, f % 2

    def flip(p):
        return jnp.where(p < nc // 2, p, 3 * nc // 2 - 1 - p)

    pos = flip(c)
    d = lax.rem(pos - flip(s) + nc, nc)
    nxt = (s, 2 * flip(lax.rem(pos + 1, nc)) + k)
    prv = (s, 2 * flip(lax.rem(pos + nc - 1, nc)) + k)
    sib = (s, 2 * c + 1 - k)
    width = wt.shape[1]
    tile = min(256, width)

    own = pltpu.make_async_copy(x_ref, col.at[s], own_sem)
    own.start()
    acc_ref[...] = jnp.zeros_like(acc_ref)
    grad_ref[...] = jnp.zeros_like(grad_ref)

    barrier = pltpu.get_barrier_semaphore()
    for dev in (nxt, prv, sib):
        pl.semaphore_signal(barrier, inc=1, device_id=dev, device_id_type=MESH)

    @pl.when(s > 0)
    def _():
        pl.semaphore_signal(barrier, inc=1, device_id=(s - 1, f), device_id_type=MESH)

    @pl.when(s < nz - 1)
    def _():
        pl.semaphore_signal(barrier, inc=1, device_id=(s + 1, f), device_id_type=MESH)

    pl.semaphore_wait(barrier, 3 + (s > 0).astype(jnp.int32) + (s < nz - 1).astype(jnp.int32))
    own.wait()

    def z_copy(o, i, way):
        return pltpu.make_async_remote_copy(
            col.at[o, i], col.at[o, i], z_send.at[o, i, way], z_recv.at[o, i],
            device_id=(s + 1 - 2 * way, f), device_id_type=MESH)

    def ring_copy(src, o, i, dev):
        return pltpu.make_async_remote_copy(
            src.at[o, i], row.at[k, o, i], ring_send.at[o, i], ring_recv.at[o, i],
            device_id=dev, device_id_type=MESH)

    def sib_copy(src, o, i):
        return pltpu.make_async_remote_copy(
            src.at[o, i], row.at[k, o, i], sib_send.at[o, i], sib_recv.at[o, i],
            device_id=sib, device_id_type=MESH)

    def sib_wait(o, i):
        pltpu.make_async_remote_copy(
            row.at[1 - k, o, i], row.at[1 - k, o, i], sib_send.at[o, i], sib_recv.at[o, i],
            device_id=sib, device_id_type=MESH).wait_recv()

    def loc_copy(o, i):
        return pltpu.make_async_copy(col.at[o, i], row.at[k, o, i], loc_sem.at[o, i])

    def send_own(i):
        @pl.when(s < nz - 1)
        def _():
            z_copy(s, i, 0).start()

        @pl.when(s > 0)
        def _():
            z_copy(s, i, 1).start()

    def is_cw(o, i):
        return lax.rem(i + (o > s).astype(jnp.int32), 2) == 0

    def spread(o, i):
        @pl.when(d == 0)
        def _():
            cw = is_cw(o, i)

            @pl.when(cw)
            def _():
                ring_copy(col, o, i, nxt).start()

            @pl.when(jnp.logical_not(cw))
            def _():
                ring_copy(col, o, i, prv).start()

            sib_copy(col, o, i).start()
            loc_copy(o, i).start()

    def passing(o, i, cw):
        @pl.when(is_cw(o, i) == cw)
        def _():
            mine = row.at[k]
            ring_copy(mine, o, i, nxt).wait_recv()
            if cw:
                @pl.when(d < nc - 1)
                def _():
                    ring_copy(mine, o, i, nxt).start()
            else:
                @pl.when(d > 1)
                def _():
                    ring_copy(mine, o, i, prv).start()
            sib_copy(mine, o, i).start()

    def compute(o, i):
        sib_wait(o, i)

        @pl.when(d == 0)
        def _():
            loc_copy(o, i).wait()

        block = col[o, i]
        wt[...] = (block.astype(jnp.float32) * w_ref[o, i]).astype(jnp.bfloat16)
        grad_ref[...] += jnp.dot(r_ref[o, i], block, preferred_element_type=jnp.float32)
        for kk in range(2):
            @pl.loop(0, width // tile)
            def _(m):
                at = pl.multiple_of(m * tile, tile)
                lhs = row[kk, o, i, :, pl.ds(at, tile)]
                acc_ref[pl.ds(kk * width + at, tile), :] += lax.dot_general(
                    lhs, wt[...], (((0,), (0,)), ((), ())), preferred_element_type=jnp.float32)

    steps = (nz - 1) * nch

    def events(e, fn):
        @pl.when(jnp.logical_and(e >= 0, e < steps))
        def _():
            j = e // nch + 1
            i = e % nch

            @pl.when(j == 1)
            def _():
                fn(s, i)

            @pl.when(s - j >= 0)
            def _():
                fn(s - j, i)

            @pl.when(s + j < nz)
            def _():
                fn(s + j, i)

    def arrive(o, i):
        @pl.when(o != s)
        def _():
            z_copy(o, i, 0).wait_recv()

            @pl.when(jnp.logical_and(o < s, s < nz - 1))
            def _():
                z_copy(o, i, 0).start()

            @pl.when(jnp.logical_and(o > s, s > 0))
            def _():
                z_copy(o, i, 1).start()
        spread(o, i)

    send_own(0)

    @pl.loop(0, steps + nc)
    def _(t):
        @pl.when(t + 1 < nch)
        def _():
            send_own(t + 1)
        events(t, arrive)

        @pl.when(d > 0)
        def _():
            events(t - d, lambda o, i: passing(o, i, True))
            events(t - (nc - d), lambda o, i: passing(o, i, False))
        events(t - nc, compute)

    @pl.loop(0, nz * nch)
    def _(q):
        o = q // nch
        i = q % nch

        @pl.when(jnp.logical_and(o <= s, s < nz - 1))
        def _():
            z_copy(o, i, 0).wait_send()

        @pl.when(jnp.logical_and(o >= s, s > 0))
        def _():
            z_copy(o, i, 1).wait_send()

        sib_copy(row.at[k], o, i).wait_send()
        cw = is_cw(o, i)

        @pl.when(jnp.logical_or(jnp.logical_and(cw, d < nc - 1),
                                jnp.logical_and(jnp.logical_not(cw), d != 1)))
        def _():
            ring_copy(row.at[k], o, i, nxt).wait_send()


def per_device(nz, nf, design, labels, coef_all, active, penalty):
    rows, width = design.shape
    nc = nf // 2
    nch = 4
    ch = rows // nch
    scale = 1.0 / jnp.sqrt(jnp.float32(rows * nz))
    beta = coef_all[active]
    partial_margin = jnp.dot(design, beta.astype(jnp.bfloat16), preferred_element_type=jnp.float32)
    margin = lax.psum(partial_margin, "feat")
    prob = 1.0 / (1.0 + jnp.exp(-margin))
    weight = prob * (1.0 - prob)
    resid = prob - labels.astype(jnp.float32)
    both = lax.all_gather(jnp.stack([weight, resid]), "samp", axis=0)
    w4 = both[:, 0].reshape(nz, nch, ch, 1)
    r4 = jnp.broadcast_to(both[:, 1].astype(jnp.bfloat16).reshape(nz, nch, 1, ch), (nz, nch, 16, ch))
    vmem = pl.BlockSpec(memory_space=pltpu.VMEM)
    dma = pltpu.SemaphoreType.DMA
    terms, grad = pl.pallas_call(
        functools.partial(kernel, nz, nc, nch),
        out_shape=(jax.ShapeDtypeStruct((2 * width, width), jnp.float32),
                   jax.ShapeDtypeStruct((16, width), jnp.float32)),
        in_specs=[pl.BlockSpec(memory_space=pl.ANY), vmem, vmem],
        out_specs=(vmem, vmem),
        scratch_shapes=[
            pltpu.VMEM((nz, nch, ch, width), jnp.bfloat16),
            pltpu.VMEM((2, nz, nch, ch, width), jnp.bfloat16),
            pltpu.VMEM((ch, width), jnp.bfloat16),
            dma,
            dma((nz, nch, 2)),
            dma((nz, nch)),
            dma((nz, nch)),
            dma((nz, nch)),
            dma((nz, nch)),
            dma((nz, nch)),
            dma((nz, nch)),
        ],
        compiler_params=pltpu.CompilerParams(
            collective_id=0, has_side_effects=True, vmem_limit_bytes=60 * 1024 * 1024),
        cost_estimate=pl.CostEstimate(
            flops=4 * nz * rows * width * width, bytes_accessed=2 * rows * width + 8 * width * width,
            transcendentals=0),
    )(design.reshape(nch, ch, width), w4, r4)
    return terms * scale, grad[0] * scale + penalty * beta


def solution(mesh):
    in_specs = (P("samp", "feat"), P("samp"), P(), P("feat"), P("feat"))
    out_specs = (P("samp", "feat"), P("feat"))
    return jax.shard_map(
        functools.partial(per_device, mesh.shape["samp"], mesh.shape["feat"]),
        mesh=mesh, in_specs=in_specs, out_specs=out_specs, check_vma=False
    )
```
